32 devices in a mesh: gx: 8 (over y, x, core), gy: 4 (over z).
Axes of the slice: x: 2, y: 2, z: 4, core: 2. Of those that a mesh axis runs over, the one named last changes fastest.
Arguments:
- leaf_load: bfloat16 [65536, 384], P(('gx', 'gy')), may hold values from -6 to 6
- front_zero: bfloat16 [65536, 8192], P(('gx', 'gy')), may hold values from -0.046875 to 0.046875
- front_one: bfloat16 [32768, 8192], P(('gx', 'gy')), may hold values from -0.046875 to 0.046875
- front_two: bfloat16 [16384, 8192], P(('gx', 'gy')), may hold values from -0.046875 to 0.046875
- front_root: bfloat16 [8192, 8192], P(('gx', 'gy')), may hold values from -0.046875 to 0.046875
- load_one: float32 [32768, 384], P(('gx', 'gy')), may hold values from -6 to 6
- load_two: float32 [16384, 384], P(('gx', 'gy')), may hold values from -6 to 6
- load_root: float32 [8192, 384], P(('gx', 'gy')), may hold values from -6 to 6
- map_one: int32 [8192, 2], replicated, may hold values from 0 to 2047
- map_two: int32 [8192, 2], replicated, may hold values from 0 to 1023
- map_root: int32 [8192, 2], replicated, may hold values from 0 to 511
- adjoint: float32 [128, 64, 384], P('gx', 'gy'), may hold values from -6 to 6
Outputs:
- root_solution: float32 [8192, 384], P(('gx', 'gy'))
- gradient: float32 [128, 64, 384], P('gx', 'gy')
The draws below stay inside these ranges and needn't reach their ends.
All inputs are finite; a program needn't handle non-finite values.
Results may differ from the reference program's by a relative error of at most 0.0055.
Values may be sent and summed in bfloat16 or wider, within the bound.
A program may use at most 128 MiB of HBM per device.

```python
import jax
import jax.numpy as jnp
from jax import lax

FRONT = 8192
CASES = 384
LEAF_BITS = 0
ROWS0 = 2048
PY = 16
PX = 16
NX = 128
NY = 64
N_GX = 8
N_GY = 4


def touch_ends(result, stream_key, least, top_value):
    spot = [jax.random.randint(jax.random.fold_in(stream_key, axis), (), 0, length) for axis, length in enumerate(result.shape)]
    widest = result.shape.index(max(result.shape))
    neighbour = spot[:widest] + [(spot[widest] + 1) % result.shape[widest]] + spot[widest + 1:]
    return result.at[tuple(spot)].set(least).at[tuple(neighbour)].set(top_value)


def block_levels(own_key, dims, cuts, low, high):
    gain, own = 1.0, jax.random.fold_in(own_key, 6)
    for axis_at, blocks in cuts:
        heights = jnp.exp(jax.random.uniform(jax.random.fold_in(own, axis_at), (blocks,), jnp.float32, low / len(cuts), high / len(cuts)))
        gain = gain * jnp.repeat(heights, dims[axis_at] // blocks).reshape([-1 if axis == axis_at else 1 for axis in range(len(dims))])
    return gain


def centred(key, shape, width, most, pieces=(), held_as=jnp.bfloat16):
    result = jax.random.normal(key, shape, jnp.float32) * width
    if len(pieces) > 0:
        result = block_levels(key, shape, pieces, -0.22, 0.18) * result
    return jnp.clip(result, min=-most, max=most).astype(held_as)


def setup_inputs(seed: int = 0) -> dict:
    keys = jax.random.split(jax.random.key(seed), 13)
    return {
        "leaf_load": centred(keys[0], (8 * FRONT, CASES), 1.0, 6.0, ((0, 32),)),
        "front_zero": centred(keys[1], (8 * FRONT, FRONT), (2 * FRONT) ** -0.5, 0.046875, ((0, 32),)),
        "front_one": centred(keys[2], (4 * FRONT, FRONT), (2 * FRONT) ** -0.5, 0.046875, ((0, 32),)),
        "front_two": centred(keys[3], (2 * FRONT, FRONT), (2 * FRONT) ** -0.5, 0.046875, ((0, 32),)),
        "front_root": centred(keys[4], (FRONT, FRONT), (2 * FRONT) ** -0.5, 0.046875, ((0, 32),)),
        "load_one": centred(keys[5], (4 * FRONT, CASES), 1.0, 6.0, ((0, 32),), jnp.float32),
        "load_two": centred(keys[6], (2 * FRONT, CASES), 1.0, 6.0, ((0, 32),), jnp.float32),
        "load_root": centred(keys[7], (FRONT, CASES), 1.0, 6.0, ((0, 32),), jnp.float32),
        "map_one": touch_ends(jax.random.randint(keys[8], (FRONT, 2), 0, ROWS0), jax.random.fold_in(keys[8], 1), 0, ROWS0 - 1).astype(jnp.int32),
        "map_two": touch_ends(jax.random.randint(keys[9], (FRONT, 2), 0, ROWS0 // 2), jax.random.fold_in(keys[9], 1), 0, (ROWS0 // 2) - 1).astype(jnp.int32),
        "map_root": touch_ends(jax.random.randint(keys[10], (FRONT, 2), 0, ROWS0 // 4), jax.random.fold_in(keys[10], 1), 0, (ROWS0 // 4) - 1).astype(jnp.int32),
        "adjoint": centred(keys[11], (NX, NY, CASES), 1.0, 6.0, ((0, 8), (1, 4)), jnp.float32),
    }


def apply_level(front, state):
    count = front.shape[0] // FRONT
    blocks = front.reshape(count, FRONT, FRONT)
    values = state.reshape(count, FRONT, CASES)
    product = lax.map(lambda pair: jnp.dot(pair[0], pair[1], preferred_element_type=jnp.float32), (blocks, values))
    return product.reshape(count * FRONT, CASES)


def extend(product, load, mapping, level):
    bit = LEAF_BITS + level
    span = 2 ** bit
    rows = product.shape[0] // (N_GX * N_GY)
    half = rows // 2
    outer = N_GX // (2 * span)
    full = (outer, 2, span, N_GY, rows, CASES)
    shape = (outer, 2, span, N_GY, half, CASES)
    six = product.reshape(full)
    first = jnp.broadcast_to(six[:, 0:1], full)
    second = jnp.broadcast_to(six[:, 1:2], full)
    index = mapping.reshape(1, 2, span, N_GY, half, 2).astype(jnp.int32)
    index_a = jnp.broadcast_to(index[..., 0:1], shape)
    index_b = jnp.broadcast_to(index[..., 1:2], shape)
    picked_a = jnp.take_along_axis(first, index_a, axis=4)
    picked_b = jnp.take_along_axis(second, index_b, axis=4)
    total = load.reshape(shape) + picked_a + picked_b
    return total.astype(jnp.bfloat16).reshape(outer * 2 * span * N_GY * half, CASES)


def reference(leaf_load, front_zero, front_one, front_two, front_root, load_one, load_two, load_root, map_one, map_two, map_root, adjoint):
    fronts = (front_zero, front_one, front_two, front_root)
    loads = (load_one, load_two, load_root)
    mappings = (map_one, map_two, map_root)
    state = leaf_load
    for level in range(3):
        product = apply_level(fronts[level], state)
        state = extend(product, loads[level], mappings[level], level)
    root_solution = apply_level(front_root, state)
    plane = root_solution.reshape(N_GX, N_GY, PX, PY, CASES).transpose(0, 2, 1, 3, 4).reshape(NX, NY, CASES)
    padded_u = jnp.pad(plane, ((1, 1), (1, 1), (0, 0)))
    padded_a = jnp.pad(adjoint, ((1, 1), (1, 1), (0, 0)))
    gradient = jnp.zeros((NX, NY, CASES), jnp.float32)
    for lo_x, lo_y in ((2, 1), (0, 1), (1, 2), (1, 0)):
        near_u = padded_u[lo_x:lo_x + NX, lo_y:lo_y + NY]
        near_a = padded_a[lo_x:lo_x + NX, lo_y:lo_y + NY]
        gradient = gradient + (plane - near_u) * (adjoint - near_a)
    return root_solution, gradient
```

```python
import functools

import jax
import jax.numpy as jnp
from jax import lax
from jax.experimental import pallas as pl
from jax.experimental.pallas import tpu as pltpu
from jax.sharding import PartitionSpec as P

MESH = pl.DeviceIdType.MESH
CHUNK = 128
LINK = 92e3
PAIR = 500e3


class Plan:
    def __init__(self):
        self.now = 0.0
        self.free = {}

    def send(self, link, size, rate):
        begin = max(self.now, self.free.get(link, 0.0))
        self.free[link] = begin + size / rate
        return self.free[link] + 1.0


def count_copies(n, leaf_bits, chunks):
    total = 0
    for level in range(4):
        bits = leaf_bits + level
        total += chunks * (2 * (n - 1) + bits * (2 * n - 1) + 2**bits + 1)
    return total


def kernel(
    n, gx, leaf_ref, f0, f1, f2, f3, l1, l2, l3, p1, p2, p3, out_ref,
    z0, z1, z2, z3, s1, s2, s3, r1, r2, r3, k1, k2, k3, w_ref, a_ref, a_sem, send_sems, recv_sems,
):
    fronts, loads, picks = (f0, f1, f2, f3), (l1, l2, l3), (p1, p2, p3)
    zs, sends, recvs, keeps = (z0, z1, z2, z3), (s1, s2, s3), (r1, r2, r3), (k1, k2, k3)
    gx_bits = gx.bit_length() - 1
    leaf_bits = gx_bits - 3
    chunks = out_ref.shape[1] // CHUNK
    column, line = lax.axis_index("gx"), lax.axis_index("gy")
    digit = [(column // 2**b) % 2 for b in range(gx_bits)]
    partner = [column + (1 - 2 * digit[b]) * 2**b for b in range(gx_bits)]
    plan = Plan()
    used = [0]
    open_sends = []

    barrier = pltpu.get_barrier_semaphore()
    for b in range(gx_bits):
        pl.semaphore_signal(barrier, inc=1, device_id={"gx": partner[b]}, device_id_type=MESH)

    @pl.when(line > 0)
    def _():
        pl.semaphore_signal(barrier, inc=1, device_id={"gy": line - 1}, device_id_type=MESH)

    @pl.when(line < n - 1)
    def _():
        pl.semaphore_signal(barrier, inc=1, device_id={"gy": line + 1}, device_id_type=MESH)

    neighbours = jnp.minimum(line, 1) + jnp.minimum(n - 1 - line, 1)
    pl.semaphore_wait(barrier, gx_bits + neighbours)

    def guarded(cond, act):
        if cond is None:
            act()
        else:
            pl.when(cond)(act)

    def transfer(src, dst, target, cond=None, recv_cond=None):
        slot = used[0]
        used[0] += 1

        def make():
            return pltpu.make_async_remote_copy(
                src_ref=src, dst_ref=dst, send_sem=send_sems.at[slot], recv_sem=recv_sems.at[slot],
                device_id=target, device_id_type=MESH,
            )

        guarded(cond, lambda: make().start())
        open_sends.append((cond, lambda: make().wait_send()))
        return lambda: guarded(recv_cond, lambda: make().wait_recv())

    parity = [0]

    def tile_rows(level):
        return min(256, fronts[level].shape[0])

    def tile_copy(level, tile, slot):
        rows = tile_rows(level)
        return pltpu.make_async_copy(
            fronts[level].at[pl.ds(pl.multiple_of(tile * rows, rows), rows), :],
            a_ref.at[slot, pl.ds(0, rows), :],
            a_sem.at[slot],
        )

    def matmul(level, chunk):
        rows = tile_rows(level)
        tiles = fronts[level].shape[0] // rows
        base = parity[0]
        parity[0] = (base + tiles) % 2
        tile_copy(level, 0, base).start()

        def body(tile, _):
            slot = (base + tile) % 2

            @pl.when(tile + 1 < tiles)
            def _():
                tile_copy(level, tile + 1, (base + tile + 1) % 2).start()

            tile_copy(level, tile, slot).wait()
            product = jnp.dot(
                a_ref[slot, :rows, :], zs[level][chunk], preferred_element_type=jnp.float32
            )
            at = pl.ds(pl.multiple_of(tile * rows, rows), rows)
            if level < 3:
                high = product.astype(jnp.bfloat16)
                low = (product - high.astype(jnp.float32)).astype(jnp.bfloat16)
                w_ref[at, :CHUNK] = high
                w_ref[at, CHUNK:] = low
            else:
                out_ref[at, chunk * CHUNK : (chunk + 1) * CHUNK] = product
            return 0

        lax.fori_loop(0, tiles, body, 0)
        plan.now += tiles * rows / 256 * 1.3 + 1.0

    def pick(level, chunk):
        depth = fronts[level].shape[0]
        half = depth // 2
        rows = min(256, half)
        tiles = half // rows
        cols = pl.ds(chunk * CHUNK, CHUNK)

        def chosen(at, width):
            lanes = lax.broadcasted_iota(jnp.int32, (rows, depth), 1)
            hot = jnp.where(lanes == picks[level][at, :], 1.0, 0.0).astype(jnp.bfloat16)
            return jnp.dot(hot, w_ref[:depth, :width], preferred_element_type=jnp.float32)

        def outgoing(tile, _):
            at = pl.ds(pl.multiple_of(half + tile * rows, rows), rows)
            to = pl.ds(pl.multiple_of(tile * rows, rows), rows)
            sends[level][chunk, to, :] = chosen(at, CHUNK).astype(jnp.bfloat16)
            return 0

        def staying(tile, _):
            at = pl.ds(pl.multiple_of(tile * rows, rows), rows)
            both = chosen(at, 2 * CHUNK)
            keeps[level][chunk, at, :] = loads[level][at, cols] + (
                both[:, :CHUNK] + both[:, CHUNK:]
            )
            return 0

        lax.fori_loop(0, tiles, outgoing, 0)
        plan.now += tiles * 0.5 * depth / 2048
        b = leaf_bits + level
        landed = transfer(
            sends[level].at[chunk], recvs[level].at[chunk], {"gx": partner[b]}
        )
        size = half * CHUNK * 2
        ready = plan.send(b, size * (1 if b == 0 else 2), PAIR if b == 0 else LINK)
        lax.fori_loop(0, tiles, staying, 0)
        plan.now += tiles * 0.6 * depth / 2048
        return landed, ready

    def stream(chunk):
        cols = pl.ds(chunk * CHUNK, CHUNK)
        for level in range(4):
            rows = fronts[level].shape[0]
            bits = leaf_bits + level
            order = list(range(1, bits)) + ([0] if bits else [])
            buf = zs[level]
            size = rows * CHUNK * 2
            group = column % 2**bits

            def shard(index, block=None):
                block = group if block is None else block
                start = (block * n + index) * rows
                return buf.at[chunk, pl.ds(pl.multiple_of(start, rows), rows), :]

            def span(block):
                start = block * n * rows
                return buf.at[chunk, pl.ds(pl.multiple_of(start, rows), n * rows), :]

            def flipped(mask):
                block = group
                for b in range(bits):
                    if mask >> b & 1:
                        block = block + (1 - 2 * digit[b]) * 2**b
                return block

            if level == 0:
                own = pl.ds(pl.multiple_of((group * n + line) * rows, rows), rows)
                buf[chunk, own, :] = leaf_ref[:, cols]
            across = {b: [] for b in order}
            arrive = {b: 0.0 for b in order}

            def share(index, cond):
                for b in order:
                    across[b].append(
                        transfer(shard(index), shard(index), {"gx": partner[b]}, cond, cond)
                    )
                    arrive[b] = plan.send(
                        b, size * (1 if b == 0 else 2), PAIR if b == 0 else LINK
                    )

            def forward(step):
                up = transfer(
                    shard(line - step + 1), shard(line - step + 1), {"gy": line + 1},
                    (line - step + 1 >= 0) & (line < n - 1), line >= step,
                )
                down = transfer(
                    shard(line + step - 1), shard(line + step - 1), {"gy": line - 1},
                    (line + step - 1 < n) & (line > 0), line + step < n,
                )
                return up, down, plan.send("z", 2 * size, LINK)

            up, down, ready = forward(1)
            share(line, None)
            for step in range(1, n):
                yield ready
                up()
                down()
                if step < n - 1:
                    up, down, ready = forward(step + 1)
                share(line - step, line >= step)
                share(line + step, line + step < n)
            pending = {1 << b: (across[b], arrive[b], at) for at, b in enumerate(order)}
            while pending:
                mask = min(pending, key=lambda m: (pending[m][1], m))
                waits, ready, at = pending.pop(mask)
                yield ready
                for wait in waits:
                    wait()
                for later in range(at + 1, len(order)):
                    b = order[later]
                    got = transfer(
                        span(flipped(mask)), span(flipped(mask)), {"gx": partner[b]}
                    )
                    when = plan.send(
                        b, n * size * (1 if b == 0 else 2), PAIR if b == 0 else LINK
                    )
                    pending[mask | 1 << b] = ([got], when, later)
            matmul(level, chunk)
            if level < 3:
                yield plan.now
                landed, ready = pick(level, chunk)
                yield ready
                landed()
                rows = rows // 2
                group = column % 2 ** (bits + 1)
                own = pl.ds(pl.multiple_of((group * n + line) * rows, rows), rows)
                zs[level + 1][chunk, own, :] = (
                    keeps[level][chunk] + recvs[level][chunk].astype(jnp.float32)
                ).astype(jnp.bfloat16)

    lead = 2 * leaf_ref.shape[0] * CHUNK * 2 / LINK
    waiting = []
    for chunk in range(chunks):
        waiting.append([0.0 if chunk < 2 else 3.5 * lead, chunk, stream(chunk)])
    while waiting:
        entry = min(waiting, key=lambda e: (e[0], e[1]))
        plan.now = max(plan.now, entry[0])
        try:
            entry[0] = next(entry[2])
        except StopIteration:
            waiting.remove(entry)
    for cond, wait in open_sends:
        guarded(cond, wait)


def halos(cells):
    sides = []
    for axis, dim in (("gx", 0), ("gy", 1)):
        count = lax.axis_size(axis)
        head = lax.slice_in_dim(cells, 0, 1, axis=dim)
        tail = lax.slice_in_dim(cells, cells.shape[dim] - 1, cells.shape[dim], axis=dim)
        sides.append(lax.ppermute(tail, axis, [(i, i + 1) for i in range(count - 1)]))
        sides.append(lax.ppermute(head, axis, [(i + 1, i) for i in range(count - 1)]))
    return sides


def local(
    leaf_load, front_zero, front_one, front_two, front_root, load_one, load_two, load_root,
    map_one, map_two, map_root, adjoint,
):
    gx, n = lax.axis_size("gx"), lax.axis_size("gy")
    leaf_bits = gx.bit_length() - 4
    column, line = lax.axis_index("gx"), lax.axis_index("gy")
    rows0, cases = leaf_load.shape
    chunks = cases // CHUNK
    front = front_zero.shape[1]
    picks = []
    for level, mapping in enumerate((map_one, map_two, map_root)):
        bits = leaf_bits + level
        half = rows0 >> level + 1
        upper = column >> bits & 1
        rows = []
        for owner in (column, column ^ 1 << bits):
            position = owner % 2 ** (bits + 1) * n + line
            rows.append(lax.dynamic_slice(mapping, (position * half, upper), (half, 1)))
        picks.append(jnp.concatenate(rows, 0))
    vmem = pl.BlockSpec(memory_space=pltpu.VMEM)
    hbm = pl.BlockSpec(memory_space=pl.ANY)
    halves = [rows0 >> k for k in (1, 2, 3)]
    copies = count_copies(n, leaf_bits, chunks)
    root_solution = pl.pallas_call(
        functools.partial(kernel, n, gx),
        out_shape=jax.ShapeDtypeStruct((rows0 // 8, cases), jnp.float32),
        in_specs=[vmem] + [hbm] * 4 + [vmem] * 6,
        out_specs=vmem,
        scratch_shapes=[pltpu.VMEM((chunks, front, CHUNK), jnp.bfloat16)] * 4
        + [pltpu.VMEM((chunks, half, CHUNK), jnp.bfloat16) for half in halves] * 2
        + [pltpu.VMEM((chunks, half, CHUNK), jnp.float32) for half in halves]
        + [
            pltpu.VMEM((rows0, 2 * CHUNK), jnp.bfloat16),
            pltpu.VMEM((2, min(256, rows0), front), jnp.bfloat16),
            pltpu.SemaphoreType.DMA((2,)),
            pltpu.SemaphoreType.DMA((copies,)),
            pltpu.SemaphoreType.DMA((copies,)),
        ],
        compiler_params=pltpu.CompilerParams(
            collective_id=0, has_side_effects=True, vmem_limit_bytes=60 * 2**20
        ),
        cost_estimate=pl.CostEstimate(
            flops=30 * rows0 // 8 * front * cases, bytes_accessed=180_000_000, transcendentals=0
        ),
    )(leaf_load, front_zero, front_one, front_two, front_root, load_one, load_two, load_root, *picks)
    plane = root_solution.reshape(adjoint.shape)
    near_a = halos(adjoint)
    near_u = halos(plane)

    def moved(cells, sides):
        return (
            jnp.concatenate([sides[0], cells[:-1]], 0),
            jnp.concatenate([cells[1:], sides[1]], 0),
            jnp.concatenate([sides[2], cells[:, :-1]], 1),
            jnp.concatenate([cells[:, 1:], sides[3]], 1),
        )

    gradient = jnp.zeros_like(plane)
    for u, a in zip(moved(plane, near_u), moved(adjoint, near_a)):
        gradient = gradient + (plane - u) * (adjoint - a)
    return root_solution, gradient


def solution(mesh):
    rows = P(("gx", "gy"), None)
    cells = P("gx", "gy", None)
    return jax.shard_map(
        local,
        mesh=mesh,
        in_specs=(rows,) * 8 + (P(),) * 3 + (cells,),
        out_specs=(rows, cells),
        check_vma=False,
    )
```

```python
import functools

import jax
import jax.numpy as jnp
from jax import lax
from jax.experimental import pallas as pl
from jax.experimental.pallas import tpu as pltpu
from jax.sharding import PartitionSpec as P

MESH = pl.DeviceIdType.MESH
CHUNK = 128
LINK = 92e3
PAIR = 500e3


class Plan:
    def __init__(self):
        self.now = 0.0
        self.free = {}

    def send(self, link, size, rate):
        begin = max(self.now, self.free.get(link, 0.0))
        self.free[link] = begin + size / rate
        return self.free[link] + 1.0


def count_copies(n, leaf_bits, chunks):
    total = 0
    for level in range(4):
        bits = leaf_bits + level
        total += chunks * (2 * (n - 1) + bits * (2 * n - 1) + 2**bits + 1)
    total += chunks * 8
    return total


def kernel(
    n, gx, leaf_ref, f0, f1, f2, f3, l1, l2, l3, p1, p2, p3, adj_ref, out_ref, grad_ref,
    z0, z1, z2, z3, s1, s2, s3, r1, r2, r3, k1, k2, k3, w_ref, u_pad, adj_pad, a_ref, a_sem, send_sems, recv_sems,
):
    fronts, loads, picks = (f0, f1, f2, f3), (l1, l2, l3), (p1, p2, p3)
    zs, sends, recvs, keeps = (z0, z1, z2, z3), (s1, s2, s3), (r1, r2, r3), (k1, k2, k3)
    gx_bits = gx.bit_length() - 1
    leaf_bits = gx_bits - 3
    chunks = out_ref.shape[1] // CHUNK
    column, line = lax.axis_index("gx"), lax.axis_index("gy")
    digit = [(column // 2**b) % 2 for b in range(gx_bits)]
    partner = [column + (1 - 2 * digit[b]) * 2**b for b in range(gx_bits)]
    plan = Plan()
    used = [0]
    open_sends = []

    cells_x, cells_y = adj_ref.shape[:2]
    inner = pl.ds(8, cells_y)
    u_pad[...] = jnp.zeros_like(u_pad)
    adj_pad[...] = jnp.zeros_like(adj_pad)
    for chunk in range(chunks):
        adj_pad[chunk, 1 : cells_x + 1, inner, :] = adj_ref[
            :, :, chunk * CHUNK : (chunk + 1) * CHUNK
        ]
    beside = column + 2 * digit[0] - 1
    inside = (beside >= 0) & (beside < gx)

    barrier = pltpu.get_barrier_semaphore()

    @pl.when(inside)
    def _():
        pl.semaphore_signal(barrier, inc=1, device_id={"gx": beside}, device_id_type=MESH)

    for b in range(gx_bits):
        pl.semaphore_signal(barrier, inc=1, device_id={"gx": partner[b]}, device_id_type=MESH)

    @pl.when(line > 0)
    def _():
        pl.semaphore_signal(barrier, inc=1, device_id={"gy": line - 1}, device_id_type=MESH)

    @pl.when(line < n - 1)
    def _():
        pl.semaphore_signal(barrier, inc=1, device_id={"gy": line + 1}, device_id_type=MESH)

    neighbours = jnp.minimum(line, 1) + jnp.minimum(n - 1 - line, 1)
    edge = (1 - digit[0]) * (1 - jnp.minimum(column, 1)) + digit[0] * (
        1 - jnp.minimum(gx - 1 - column, 1)
    )
    pl.semaphore_wait(barrier, gx_bits + neighbours + 1 - edge)

    def guarded(cond, act):
        if cond is None:
            act()
        else:
            pl.when(cond)(act)

    def transfer(src, dst, target, cond=None, recv_cond=None):
        slot = used[0]
        used[0] += 1

        def make():
            return pltpu.make_async_remote_copy(
                src_ref=src, dst_ref=dst, send_sem=send_sems.at[slot], recv_sem=recv_sems.at[slot],
                device_id=target, device_id_type=MESH,
            )

        guarded(cond, lambda: make().start())
        open_sends.append((cond, lambda: make().wait_send()))
        return lambda: guarded(recv_cond, lambda: make().wait_recv())

    def edges(pad, chunk):
        block = pad.at[chunk]
        own_x = pl.ds(1, cells_x)
        moves = (
            ("gx", 1, block.at[cells_x, inner], block.at[0, inner]),
            ("gx", -1, block.at[1, inner], block.at[cells_x + 1, inner]),
            ("gy", 1, block.at[own_x, pl.ds(cells_y, 8)], block.at[own_x, pl.ds(0, 8)]),
            ("gy", -1, block.at[own_x, pl.ds(8, 8)], block.at[own_x, pl.ds(cells_y + 8, 8)]),
        )
        waits = []
        for axis, hop, src, dst in moves:
            here, count = (column, gx) if axis == "gx" else (line, n)
            lower, upper = here > 0, here < count - 1
            go, come = (upper, lower) if hop == 1 else (lower, upper)
            waits.append(transfer(src, dst, {axis: here + hop}, go, come))
        return waits

    parity = [0]
    early = [None]
    busy = [False]

    def reserve(level, chunk):
        if early[0] is None:
            early[0] = (level, chunk)
            tile_copy(level, 0, 2).start()

    def tile_rows(level):
        return min(256, fronts[level].shape[0])

    def tile_copy(level, tile, slot):
        rows = tile_rows(level)
        return pltpu.make_async_copy(
            fronts[level].at[pl.ds(pl.multiple_of(tile * rows, rows), rows), :],
            a_ref.at[slot, pl.ds(0, rows), :],
            a_sem.at[slot],
        )

    def matmul(level, chunk):
        rows = tile_rows(level)
        tiles = fronts[level].shape[0] // rows
        base = parity[0]
        parity[0] = (base + tiles) % 2
        mine = early[0] == (level, chunk)
        first = 2 if mine else base
        if mine:
            early[0] = None
        else:
            tile_copy(level, 0, base).start()

        def body(tile, _):
            slot = jnp.where(tile == 0, first, (base + tile) % 2)

            @pl.when(tile + 1 < tiles)
            def _():
                tile_copy(level, tile + 1, (base + tile + 1) % 2).start()

            tile_copy(level, tile, slot).wait()
            product = jnp.dot(
                a_ref[slot, :rows, :], zs[level][chunk], preferred_element_type=jnp.float32
            )
            at = pl.ds(pl.multiple_of(tile * rows, rows), rows)
            if level < 3:
                high = product.astype(jnp.bfloat16)
                low = (product - high.astype(jnp.float32)).astype(jnp.bfloat16)
                w_ref[at, :CHUNK] = high
                w_ref[at, CHUNK:] = low
            else:
                out_ref[at, chunk * CHUNK : (chunk + 1) * CHUNK] = product
                u_pad[chunk, 1 : cells_x + 1, inner, :] = product.reshape(
                    cells_x, cells_y, CHUNK
                )
            return 0

        for begin in range(0, tiles, 2):
            end = min(begin + 2, tiles)
            lax.fori_loop(begin, end, body, 0)
            plan.now += (end - begin) * rows / 256 * 1.3 + (0.0 if mine or begin else 1.0)
            yield plan.now

    def pick(level, chunk):
        depth = fronts[level].shape[0]
        half = depth // 2
        rows = min(256, half)
        tiles = half // rows
        cols = pl.ds(chunk * CHUNK, CHUNK)

        def chosen(at, width):
            lanes = lax.broadcasted_iota(jnp.int32, (rows, depth), 1)
            hot = jnp.where(lanes == picks[level][at, :], 1.0, 0.0).astype(jnp.bfloat16)
            return jnp.dot(hot, w_ref[:depth, :width], preferred_element_type=jnp.float32)

        def outgoing(tile, _):
            at = pl.ds(pl.multiple_of(half + tile * rows, rows), rows)
            to = pl.ds(pl.multiple_of(tile * rows, rows), rows)
            sends[level][chunk, to, :] = chosen(at, CHUNK).astype(jnp.bfloat16)
            return 0

        def staying(tile, _):
            at = pl.ds(pl.multiple_of(tile * rows, rows), rows)
            both = chosen(at, 2 * CHUNK)
            keeps[level][chunk, at, :] = loads[level][at, cols] + (
                both[:, :CHUNK] + both[:, CHUNK:]
            )
            return 0

        lax.fori_loop(0, tiles, outgoing, 0)
        plan.now += tiles * 0.5 * depth / 2048
        b = leaf_bits + level
        landed = transfer(
            sends[level].at[chunk], recvs[level].at[chunk], {"gx": partner[b]}
        )
        size = half * CHUNK * 2
        ready = plan.send(b, size * (1 if b == 0 else 2), PAIR if b == 0 else LINK)
        yield plan.now
        lax.fori_loop(0, tiles, staying, 0)
        plan.now += tiles * 0.6 * depth / 2048
        return landed, ready

    def stream(chunk):
        cols = pl.ds(chunk * CHUNK, CHUNK)
        for level in range(4):
            rows = fronts[level].shape[0]
            bits = leaf_bits + level
            order = list(range(1, bits)) + ([0] if bits else [])
            buf = zs[level]
            size = rows * CHUNK * 2
            group = column % 2**bits

            def shard(index, block=None):
                block = group if block is None else block
                start = (block * n + index) * rows
                return buf.at[chunk, pl.ds(pl.multiple_of(start, rows), rows), :]

            def span(block):
                start = block * n * rows
                return buf.at[chunk, pl.ds(pl.multiple_of(start, rows), n * rows), :]

            def flipped(mask):
                block = group
                for b in range(bits):
                    if mask >> b & 1:
                        block = block + (1 - 2 * digit[b]) * 2**b
                return block

            if level == 0:
                own = pl.ds(pl.multiple_of((group * n + line) * rows, rows), rows)
                buf[chunk, own, :] = leaf_ref[:, cols]
            across = {b: [] for b in order}
            arrive = {b: 0.0 for b in order}

            def share(index, cond):
                for b in order:
                    across[b].append(
                        transfer(shard(index), shard(index), {"gx": partner[b]}, cond, cond)
                    )
                    arrive[b] = plan.send(
                        b, size * (1 if b == 0 else 2), PAIR if b == 0 else LINK
                    )

            def forward(step):
                up = transfer(
                    shard(line - step + 1), shard(line - step + 1), {"gy": line + 1},
                    (line - step + 1 >= 0) & (line < n - 1), line >= step,
                )
                down = transfer(
                    shard(line + step - 1), shard(line + step - 1), {"gy": line - 1},
                    (line + step - 1 < n) & (line > 0), line + step < n,
                )
                return up, down, plan.send("z", 2 * size, LINK)

            up, down, ready = forward(1)
            share(line, None)
            for step in range(1, n):
                if step == n - 1 and not bits:
                    reserve(level, chunk)
                yield ready
                up()
                down()
                if step < n - 1:
                    up, down, ready = forward(step + 1)
                share(line - step, line >= step)
                share(line + step, line + step < n)
            pending = {1 << b: (across[b], arrive[b], at) for at, b in enumerate(order)}
            while pending:
                mask = min(pending, key=lambda m: (pending[m][1], m))
                waits, ready, at = pending.pop(mask)
                if not pending:
                    reserve(level, chunk)
                yield ready
                for wait in waits:
                    wait()
                for later in range(at + 1, len(order)):
                    b = order[later]
                    got = transfer(
                        span(flipped(mask)), span(flipped(mask)), {"gx": partner[b]}
                    )
                    when = plan.send(
                        b, n * size * (1 if b == 0 else 2), PAIR if b == 0 else LINK
                    )
                    pending[mask | 1 << b] = ([got], when, later)
            while busy[0]:
                yield plan.now + 0.5
            busy[0] = True
            yield from matmul(level, chunk)
            if level < 3:
                landed, ready = yield from pick(level, chunk)
            busy[0] = False
            if level < 3:
                yield ready
                landed()
                rows = rows // 2
                group = column % 2 ** (bits + 1)
                own = pl.ds(pl.multiple_of((group * n + line) * rows, rows), rows)
                zs[level + 1][chunk, own, :] = (
                    keeps[level][chunk] + recvs[level][chunk].astype(jnp.float32)
                ).astype(jnp.bfloat16)
        waits = edges(u_pad, chunk)
        yield plan.now + 3.0
        for wait in waits + adj_waits[chunk]:
            wait()

        def near(pad, x, y):
            return pad[chunk, x : x + cells_x, y : y + cells_y, :]

        u, a = near(u_pad, 1, 8), near(adj_pad, 1, 8)
        total = jnp.zeros_like(u)
        for x, y in ((2, 8), (0, 8), (1, 9), (1, 7)):
            total = total + (u - near(u_pad, x, y)) * (a - near(adj_pad, x, y))
        grad_ref[:, :, cols] = total

    adj_waits = [edges(adj_pad, chunk) for chunk in range(chunks)]
    lead = 2 * leaf_ref.shape[0] * CHUNK * 2 / LINK
    waiting = []
    for chunk in range(chunks):
        waiting.append([0.0 if chunk < 2 else 3.5 * lead, chunk, stream(chunk)])
    while waiting:
        entry = min(waiting, key=lambda e: (e[0], e[1]))
        plan.now = max(plan.now, entry[0])
        try:
            entry[0] = next(entry[2])
        except StopIteration:
            waiting.remove(entry)
    for cond, wait in open_sends:
        guarded(cond, wait)


def local(
    leaf_load, front_zero, front_one, front_two, front_root, load_one, load_two, load_root,
    map_one, map_two, map_root, adjoint,
):
    gx, n = lax.axis_size("gx"), lax.axis_size("gy")
    leaf_bits = gx.bit_length() - 4
    column, line = lax.axis_index("gx"), lax.axis_index("gy")
    rows0, cases = leaf_load.shape
    chunks = cases // CHUNK
    front = front_zero.shape[1]
    picks = []
    for level, mapping in enumerate((map_one, map_two, map_root)):
        bits = leaf_bits + level
        half = rows0 >> level + 1
        upper = column >> bits & 1
        rows = []
        for owner in (column, column ^ 1 << bits):
            position = owner % 2 ** (bits + 1) * n + line
            rows.append(lax.dynamic_slice(mapping, (position * half, upper), (half, 1)))
        picks.append(jnp.concatenate(rows, 0))
    vmem = pl.BlockSpec(memory_space=pltpu.VMEM)
    hbm = pl.BlockSpec(memory_space=pl.ANY)
    halves = [rows0 >> k for k in (1, 2, 3)]
    copies = count_copies(n, leaf_bits, chunks)
    padded = (chunks, adjoint.shape[0] + 2, adjoint.shape[1] + 16, CHUNK)
    return pl.pallas_call(
        functools.partial(kernel, n, gx),
        out_shape=(
            jax.ShapeDtypeStruct((rows0 // 8, cases), jnp.float32),
            jax.ShapeDtypeStruct(adjoint.shape, jnp.float32),
        ),
        in_specs=[vmem] + [hbm] * 4 + [vmem] * 7,
        out_specs=(vmem, vmem),
        scratch_shapes=[pltpu.VMEM((chunks, front, CHUNK), jnp.bfloat16)] * 4
        + [pltpu.VMEM((chunks, half, CHUNK), jnp.bfloat16) for half in halves] * 2
        + [pltpu.VMEM((chunks, half, CHUNK), jnp.float32) for half in halves]
        + [
            pltpu.VMEM((rows0, 2 * CHUNK), jnp.bfloat16),
            pltpu.VMEM(padded, jnp.float32),
            pltpu.VMEM(padded, jnp.float32),
            pltpu.VMEM((3, min(256, rows0), front), jnp.bfloat16),
            pltpu.SemaphoreType.DMA((3,)),
            pltpu.SemaphoreType.DMA((copies,)),
            pltpu.SemaphoreType.DMA((copies,)),
        ],
        compiler_params=pltpu.CompilerParams(
            collective_id=0, has_side_effects=True, vmem_limit_bytes=60 * 2**20
        ),
        cost_estimate=pl.CostEstimate(
            flops=30 * rows0 // 8 * front * cases, bytes_accessed=180_000_000, transcendentals=0
        ),
    )(
        leaf_load, front_zero, front_one, front_two, front_root, load_one, load_two, load_root,
        *picks, adjoint,
    )


def solution(mesh):
    rows = P(("gx", "gy"), None)
    cells = P("gx", "gy", None)
    return jax.shard_map(
        local,
        mesh=mesh,
        in_specs=(rows,) * 8 + (P(),) * 3 + (cells,),
        out_specs=(rows, cells),
        check_vma=False,
    )
```
